32 devices in a mesh: seq: 4 (over y, x), tensor: 8 (over z, core).
Axes of the slice: x: 2, y: 2, z: 4, core: 2. Of those that a mesh axis runs over, the one named last changes fastest.
Arguments:
- tokens: bfloat16 [4096, 4096], P(('seq', 'tensor')), may hold values from -36 to 36
- norm_gain: float32 [4096], replicated, may hold values from 0.1 to 1.9
- in_weight: bfloat16 [4096, 3, 4096], P(None, None, 'tensor'), may hold values from -0.09375 to 0.09375
- short_filter: float32 [3, 3, 4096], P(None, None, 'tensor'), may hold values from -3 to 3
- filter_spectrum: float32 [2, 8, 4096, 1024], P(None, 'seq', 'tensor'), may hold values from -4 to 4
- out_weight: bfloat16 [4096, 4096], P('tensor'), may hold values from -0.09375 to 0.09375
Outputs:
- mixer_out: bfloat16 [4096, 4096], P(('seq', 'tensor'))
The draws below stay inside these ranges and needn't reach their ends.
All inputs are finite; a program needn't handle non-finite values.
Results may differ from the reference program's by a relative error of at most 0.012.
Values may be sent and summed in bfloat16 or wider, within the bound.
A program may use at most 192 MiB of HBM per device.

```python
import math
import jax
import jax.numpy as jnp
from jax import lax

D = 4096
TOK_SEQ = 1024
TAPS = 3
TOKENS = 4096
FREQ_BLOCKS = 8
N_TENSOR = 8


def draw_tokens(key, part):
    key_base = jax.random.fold_in(key, 11)
    key_rows = jax.random.fold_in(key, 12)
    key_cols = jax.random.fold_in(key, 13)
    row_scale = jnp.exp(jax.random.uniform(key_rows, (TOKENS, 1), jnp.float32, math.log(0.3), math.log(3.0)))
    col_scale = jnp.exp(jax.random.uniform(key_cols, (1, D), jnp.float32, math.log(0.3), math.log(3.0)))
    base = jax.random.truncated_normal(key_base, -4.0, 4.0, (TOKENS, D), jnp.float32)
    return (base * row_scale * col_scale).astype(jnp.bfloat16)


def draw_filter_spectrum(key, part):
    key_base = jax.random.fold_in(key, 21)
    return jax.random.truncated_normal(key_base, -4.0, 4.0, (2, FREQ_BLOCKS, D, TOK_SEQ), jnp.float32)


def block_scale(key, shape, cuts, least, largest):
    def one(position, shards_of):
        steps = jax.random.uniform(jax.random.fold_in(jax.random.fold_in(key, 6), position), (shards_of,), jnp.float32, least / len(cuts), largest / len(cuts))
        return jnp.repeat(jnp.exp(steps), shape[position] // shards_of).reshape((-1,) + (1,) * (len(shape) - position - 1))

    loudness = one(*cuts[0])
    for cut in cuts[1:]:
        loudness = loudness * one(*cut)
    return loudness


def scatter_about(rng, shape, scale, reach, split=(), held_as=jnp.bfloat16):
    result = jax.random.normal(rng, shape, jnp.float32) * scale
    if len(split) > 0:
        result = block_scale(rng, shape, split, -0.22, 0.18) * result
    return jnp.clip(result, min=-reach, max=reach).astype(held_as)


def setup_inputs(seed: int = 0) -> dict:
    streams_of = jax.random.split(jax.random.key(seed), 7)
    return {
        "tokens": draw_tokens(jax.random.fold_in(streams_of[6], 71), 0),
        "norm_gain": jnp.clip(1.0 + 0.18 * jax.random.normal(streams_of[1], (D,), jnp.float32), 0.1, 1.9),
        "in_weight": scatter_about(streams_of[2], (D, 3, D), D ** -0.5, 0.09375, ((2, 8),)),
        "short_filter": scatter_about(streams_of[3], (TAPS, 3, D), 0.5, 3.0, ((2, 8),), jnp.float32),
        "filter_spectrum": draw_filter_spectrum(jax.random.fold_in(streams_of[6], 71), 0),
        "out_weight": scatter_about(streams_of[5], (D, D), D ** -0.5, 0.09375, ((0, 8),)),
    }


EPS = 1e-06

def reference(tokens, norm_gain, in_weight, short_filter, filter_spectrum, out_weight):
    inputs = tokens.astype(jnp.float32)
    square_mean = lax.optimization_barrier(jnp.mean(inputs * inputs, axis=-1, keepdims=True))
    normed = (inputs / jnp.sqrt(square_mean + EPS) * norm_gain).astype(jnp.bfloat16)
    projected = jnp.dot(normed, in_weight.reshape(D, 3 * D), preferred_element_type=jnp.float32)
    projected = projected.astype(jnp.bfloat16).reshape(TOKENS, 3, D).astype(jnp.float32)
    padded = jnp.pad(projected, ((TAPS - 1, 0), (0, 0), (0, 0)))
    short = jnp.zeros((TOKENS, 3, D), jnp.float32)
    for offset in range(TAPS):
        short = short + short_filter[offset] * padded[TAPS - 1 - offset:TAPS - 1 - offset + TOKENS]
    queries = short[:, 0]
    product = (short[:, 1] * short[:, 2]).astype(jnp.bfloat16)
    layout = filter_spectrum.transpose(0, 3, 1, 2).reshape(2, 2 * TOKENS, D)
    block_width = min(D, 512)
    pieces = []
    for begin in range(0, D, block_width):
        column = product[:, begin:begin + block_width].astype(jnp.float32)
        spectrum = jnp.fft.fft(column, n=2 * TOKENS, axis=0)
        response = lax.complex(layout[0, :, begin:begin + block_width], layout[1, :, begin:begin + block_width])
        values = jnp.real(jnp.fft.ifft(spectrum * response, axis=0))[:TOKENS]
        pieces.append(values.astype(jnp.float32))
    long_conv = jnp.concatenate(pieces, axis=1)
    gated = (queries * long_conv).astype(jnp.bfloat16)
    width = D // N_TENSOR
    total = jnp.zeros((TOKENS, D), jnp.float32)
    for member in range(N_TENSOR):
        term = jnp.dot(gated[:, member * width:(member + 1) * width], out_weight[member * width:(member + 1) * width], preferred_element_type=jnp.float32)
        rounded = lax.optimization_barrier(term.astype(jnp.bfloat16)).astype(jnp.float32)
        total = total + rounded
    return (inputs + total).astype(jnp.bfloat16)
```

```python
import functools

import jax
import jax.numpy as jnp
import numpy as np
from jax import lax
from jax.experimental import pallas as pl
from jax.experimental.pallas import tpu as pltpu
from jax.sharding import PartitionSpec as P

TAPS = 3
EPS = 1e-06
HALO = 16
COLUMNS = 256
VMEM_LIMIT = 56 * 1024 * 1024


def turn(count, total, index):
    angle = 2.0 * np.pi * ((np.asarray(count) * np.asarray(index)) % total) / total
    return np.cos(angle), np.sin(angle)


def short_kernel(seq_count, proj_ref, carried_ref, taps_ref, queries_ref, product_ref):
    width = queries_ref.shape[1]
    piece = width // seq_count

    def branch(j, begin):
        columns = pl.ds(j * width + begin, piece)
        ext = jnp.concatenate(
            [carried_ref[:, columns].astype(jnp.float32), proj_ref[:, columns].astype(jnp.float32)],
            axis=0,
        )
        taps = taps_ref[:, j, pl.ds(begin, piece)]
        total = ext[HALO:] * taps[0:1]
        for offset in range(1, TAPS):
            total = total + pltpu.roll(ext, offset, 0)[HALO:] * taps[offset : offset + 1]
        return total

    for place in range(seq_count):
        begin = place * piece
        queries_ref[:, pl.ds(begin, piece)] = branch(0, begin)
        product_ref[place] = (branch(1, begin) * branch(2, begin)).astype(jnp.bfloat16)


def short_products(projected, carried, short_filter, seq_count):
    rows, total_width = projected.shape
    width = total_width // 3
    return pl.pallas_call(
        functools.partial(short_kernel, seq_count),
        out_shape=(
            jax.ShapeDtypeStruct((rows, width), jnp.float32),
            jax.ShapeDtypeStruct((seq_count, rows, width // seq_count), jnp.bfloat16),
        ),
        in_specs=[pl.BlockSpec(memory_space=pltpu.VMEM)] * 3,
        out_specs=[pl.BlockSpec(memory_space=pltpu.VMEM)] * 2,
        compiler_params=pltpu.CompilerParams(vmem_limit_bytes=VMEM_LIMIT),
        cost_estimate=pl.CostEstimate(
            flops=20 * rows * width, bytes_accessed=12 * rows * width, transcendentals=0
        ),
        name="short_products",
    )(projected, carried, short_filter)


def mixed(terms):
    total = None
    for weight, value in terms:
        if abs(weight) < 1e-12:
            continue
        if abs(abs(weight) - 1.0) < 1e-12:
            term = value if weight > 0 else -value
        else:
            term = value * np.float32(weight)
        total = term if total is None else total + term
    return total


def conv_kernel(
    x_ref, g_ref, cos_ref, sin_ref, turn_cos_ref, turn_sin_ref, out_ref, xt, y_real, y_imag, z_real, z_imag
):
    count, rows, piece = x_ref.shape
    classes = count + 1
    freq_count = 2 * count
    total_length = freq_count * rows
    for s in range(count):
        xt[s] = x_ref[s].astype(jnp.float32).T
    for tile in range(rows // COLUMNS):
        columns = pl.ds(tile * COLUMNS, COLUMNS)
        blocks = [xt[s, :, columns] for s in range(count)]
        for r in range(classes):
            cos_r, sin_r = turn(r, freq_count, np.arange(count))
            real = mixed([(cos_r[s], blocks[s]) for s in range(count)])
            imag = mixed([(-sin_r[s], blocks[s]) for s in range(count)])
            turn_cos = turn_cos_ref[r : r + 1, columns]
            turn_sin = turn_sin_ref[r : r + 1, columns]
            if imag is None:
                turned_real, turned_imag = real * turn_cos, -(real * turn_sin)
            else:
                turned_real = real * turn_cos + imag * turn_sin
                turned_imag = imag * turn_cos - real * turn_sin
            y_real[pl.ds(r * piece, piece), columns] = turned_real.astype(jnp.bfloat16)
            y_imag[pl.ds(r * piece, piece), columns] = turned_imag.astype(jnp.bfloat16)

    def dot(a, b):
        return jnp.dot(a, b, preferred_element_type=jnp.float32)

    @pl.loop(0, rows // COLUMNS)
    def _(tile):
        columns = pl.ds(pl.multiple_of(tile * COLUMNS, COLUMNS), COLUMNS)
        table_cos, table_sin = cos_ref[:, columns], sin_ref[:, columns]
        for r in range(classes):
            place = pl.ds(r * piece, piece)
            real_in, imag_in = y_real[place], y_imag[place]
            if r == 0:
                real = dot(real_in, table_cos)
                imag = -dot(real_in, table_sin)
            else:
                real = dot(real_in, table_cos) + dot(imag_in, table_sin)
                imag = dot(imag_in, table_cos) - dot(real_in, table_sin)
            g_real = g_ref[0, r, :, columns].astype(jnp.float32)
            g_imag = g_ref[1, r, :, columns].astype(jnp.float32)
            z_real[place, columns] = (real * g_real - imag * g_imag).astype(jnp.bfloat16)
            z_imag[place, columns] = (real * g_imag + imag * g_real).astype(jnp.bfloat16)

    @pl.loop(0, rows // COLUMNS)
    def _(tile):
        columns = pl.ds(pl.multiple_of(tile * COLUMNS, COLUMNS), COLUMNS)
        table_cos, table_sin = cos_ref[:, columns], sin_ref[:, columns]
        sums = [None] * count
        for r in range(classes):
            place = pl.ds(r * piece, piece)
            real_in, imag_in = z_real[place], z_imag[place]
            real = dot(real_in, table_cos) - dot(imag_in, table_sin)
            if r == 0:
                turned_real, turned_imag = real, None
            else:
                imag = dot(imag_in, table_cos) + dot(real_in, table_sin)
                turn_cos = turn_cos_ref[r : r + 1, columns]
                turn_sin = turn_sin_ref[r : r + 1, columns]
                turned_real = real * turn_cos - imag * turn_sin
                turned_imag = imag * turn_cos + real * turn_sin
            cos_r, sin_r = turn(r, freq_count, np.arange(count))
            for s in range(count):
                terms = [(1.0, sums[s])] if sums[s] is not None else []
                terms += [(cos_r[s], turned_real), (-sin_r[s], turned_imag)]
                sums[s] = mixed(terms)
        for s in range(count):
            out_ref[s, columns, :] = (sums[s] * np.float32(1.0 / total_length)).T.astype(jnp.bfloat16)


def long_convolution(blocks, response, tables):
    count, rows, piece = blocks.shape
    classes = count + 1
    flops = (16 * classes) * piece * rows * rows
    return pl.pallas_call(
        conv_kernel,
        out_shape=jax.ShapeDtypeStruct((count, rows, piece), jnp.bfloat16),
        in_specs=[pl.BlockSpec(memory_space=pltpu.VMEM)] * 6,
        out_specs=pl.BlockSpec(memory_space=pltpu.VMEM),
        scratch_shapes=[
            pltpu.VMEM((count, piece, rows), jnp.float32),
            pltpu.VMEM((classes * piece, rows), jnp.bfloat16),
            pltpu.VMEM((classes * piece, rows), jnp.bfloat16),
            pltpu.VMEM((classes * piece, rows), jnp.bfloat16),
            pltpu.VMEM((classes * piece, rows), jnp.bfloat16),
        ],
        compiler_params=pltpu.CompilerParams(vmem_limit_bytes=VMEM_LIMIT),
        cost_estimate=pl.CostEstimate(
            flops=flops, bytes_accessed=4 * rows * rows + 4 * classes * piece * rows, transcendentals=0
        ),
        name="long_convolution",
    )(blocks, response, *tables)


def folded_response(filter_spectrum):
    sent = filter_spectrum.astype(jnp.bfloat16)
    spectrum = lax.all_to_all(sent, "seq", split_axis=2, concat_axis=1, tiled=True)
    freq_count, rows = spectrum.shape[1], spectrum.shape[3]
    half = freq_count // 2
    mirror = np.eye(rows, dtype=np.float32)[::-1]
    upper = jnp.einsum(
        "ckej,jm->ckem",
        spectrum[:, half + 1 :][:, ::-1],
        jnp.asarray(mirror, jnp.bfloat16),
        preferred_element_type=jnp.float32,
    )
    upper = upper * jnp.array([1.0, -1.0], jnp.float32)[:, None, None, None]
    middle = (spectrum[:, 1:half].astype(jnp.float32) + upper).astype(jnp.bfloat16)
    return jnp.concatenate([spectrum[:, :1], middle, spectrum[:, half : half + 1]], axis=1)


def dft_tables(rows, count):
    index = np.arange(rows)
    table_cos, table_sin = turn(index[:, None], rows, index[None, :])
    classes = np.arange(count + 1)
    turn_cos, turn_sin = turn(classes[:, None], 2 * count * rows, index[None, :])
    return (
        jnp.asarray(table_cos, jnp.bfloat16),
        jnp.asarray(table_sin, jnp.bfloat16),
        jnp.asarray(turn_cos, jnp.float32),
        jnp.asarray(turn_sin, jnp.float32),
    )


def per_device(tokens, norm_gain, in_weight, short_filter, filter_spectrum, out_weight):
    seq_count = lax.axis_size("seq")
    inputs = tokens.astype(jnp.float32)
    square_mean = jnp.mean(inputs * inputs, axis=-1, keepdims=True)
    normed = (inputs / jnp.sqrt(square_mean + EPS) * norm_gain).astype(jnp.bfloat16)
    model_width = in_weight.shape[0]
    width = in_weight.shape[2]
    gathered = lax.all_gather(normed, "tensor", axis=0, tiled=True)
    rows = gathered.shape[0]
    response = folded_response(filter_spectrum)
    tables = dft_tables(rows, seq_count)
    flat_weight = in_weight.reshape(model_width, 3 * width)
    gathered, response, flat_weight = lax.optimization_barrier((gathered, response, flat_weight))
    projected = jnp.dot(gathered, flat_weight, preferred_element_type=jnp.float32).astype(jnp.bfloat16)
    route = [(i, i + 1) for i in range(seq_count - 1)]
    carried = lax.ppermute(projected[rows - HALO :], "seq", route)
    queries, product = short_products(projected, carried, short_filter, seq_count)
    blocks = lax.all_to_all(product, "seq", split_axis=0, concat_axis=0, tiled=True)
    values = long_convolution(blocks, response, tables)
    returned = lax.all_to_all(values, "seq", split_axis=0, concat_axis=0, tiled=True)
    long_conv = returned.transpose(1, 0, 2).reshape(rows, width).astype(jnp.float32)
    gated = (queries * long_conv).astype(jnp.bfloat16)
    summed = lax.psum_scatter(
        jnp.dot(gated, out_weight, preferred_element_type=jnp.float32).astype(jnp.bfloat16),
        "tensor",
        scatter_dimension=0,
        tiled=True,
    ).astype(jnp.float32)
    return (inputs + summed).astype(jnp.bfloat16)


def solution(mesh):
    in_specs = (
        P(("seq", "tensor"), None),
        P(),
        P(None, None, "tensor"),
        P(None, None, "tensor"),
        P(None, "seq", "tensor", None),
        P("tensor", None),
    )
    out_specs = P(("seq", "tensor"), None)
    return jax.shard_map(
        per_device, mesh=mesh, in_specs=in_specs, out_specs=out_specs, check_vma=False
    )
```

```python
import functools

import jax
import jax.numpy as jnp
import numpy as np
from jax import lax
from jax.experimental import pallas as pl
from jax.experimental.pallas import tpu as pltpu
from jax.sharding import PartitionSpec as P

TAPS = 3
EPS = 1e-06
HALO = 16
COLUMNS = 256
VMEM_LIMIT = 56 * 1024 * 1024


def turn(count, total, index):
    angle = 2.0 * np.pi * ((np.asarray(count) * np.asarray(index)) % total) / total
    return np.cos(angle), np.sin(angle)


MESH = pl.DeviceIdType.MESH
CHUNKS = 4


def gather_kernel(
    seq_count, tensor_count, normed_ref, weight_ref, filter_ref, proj_ref, spectrum_ref,
    held, weights, weight_sem, own_sem, filter_send, filter_recv, recv, to_right, to_left, to_sibling,
):
    seq_place = lax.axis_index("seq")
    place = lax.axis_index("tensor")
    chips = tensor_count // 2
    chip, core = place // 2, place % 2
    sibling = chip * 2 + 1 - core
    has_right, has_left = chip < chips - 1, chip > 0
    right, left = place + 2, place - 2
    size = held.shape[1]
    step = size // CHUNKS
    classes = filter_ref.shape[1]
    piece = spectrum_ref.shape[2]
    width = weight_ref.shape[2]

    weight_copy = pltpu.make_async_copy(weight_ref, weights, weight_sem)
    weight_copy.start()
    own_filter = pltpu.make_async_copy(
        filter_ref.at[:, :, pl.ds(seq_place * piece, piece), :],
        spectrum_ref.at[:, pl.ds(seq_place * classes, classes), :, :],
        own_sem,
    )
    own_filter.start()
    held[place] = normed_ref[...]

    barrier = pltpu.get_barrier_semaphore()
    pl.semaphore_signal(barrier, inc=1, device_id={"tensor": sibling}, device_id_type=MESH)

    @pl.when(has_right)
    def _():
        pl.semaphore_signal(barrier, inc=1, device_id={"tensor": right}, device_id_type=MESH)

    @pl.when(has_left)
    def _():
        pl.semaphore_signal(barrier, inc=1, device_id={"tensor": left}, device_id_type=MESH)

    for k in range(1, seq_count):
        peer = lax.rem(seq_place + k, seq_count)
        pl.semaphore_signal(barrier, inc=1, device_id={"seq": peer}, device_id_type=MESH)
    neighbours = has_right.astype(jnp.int32) + has_left.astype(jnp.int32)
    pl.semaphore_wait(barrier, seq_count + neighbours)

    def passed(block, q, target, send_sem):
        part = held.at[block, pl.ds(q * step, step)]
        return pltpu.make_async_remote_copy(
            src_ref=part,
            dst_ref=part,
            send_sem=send_sem.at[block, q],
            recv_sem=recv.at[block, q],
            device_id={"tensor": target},
            device_id_type=MESH,
        )

    def filter_copy(k):
        peer = lax.rem(seq_place + k, seq_count)
        return pltpu.make_async_remote_copy(
            src_ref=filter_ref.at[:, :, pl.ds(peer * piece, piece), :],
            dst_ref=spectrum_ref.at[:, pl.ds(seq_place * classes, classes), :, :],
            send_sem=filter_send.at[k],
            recv_sem=filter_recv.at[k],
            device_id={"seq": peer},
            device_id_type=MESH,
        )

    def multiply(other):
        for q in range(CHUNKS):
            passed(other * 2 + 1 - core, q, sibling, to_sibling).wait_recv()
        rows = pl.ds(pl.multiple_of(other * 2 * size, 2 * size), 2 * size)

        @pl.loop(0, 3)
        def _(j):
            for begin in range(0, width, 256):
                columns = min(256, width - begin)
                value = jnp.dot(
                    held[pl.ds(other * 2, 2)].reshape(2 * size, held.shape[2]),
                    weights[j, :, pl.ds(begin, columns)],
                    preferred_element_type=jnp.float32,
                )
                proj_ref[j, rows, pl.ds(begin, columns)] = value.astype(jnp.bfloat16)

    for q in range(CHUNKS):

        @pl.when(has_right)
        def _():
            passed(place, q, right, to_right).start()

        @pl.when(has_left)
        def _():
            passed(place, q, left, to_left).start()

        passed(place, q, sibling, to_sibling).start()
    for k in range(1, seq_count):
        filter_copy(k).start()
    weight_copy.wait()
    multiply(chip)

    def sides(distance):
        yield chip + distance, chip + distance < chips, right, has_left, left, to_left
        yield chip - distance, chip - distance >= 0, left, has_right, right, to_right

    @pl.loop(1, chips)
    def _(distance):
        for q in range(CHUNKS):
            for other, exists, source, onward, target, send_sem in sides(distance):

                @pl.when(exists)
                def _():
                    block = other * 2 + core
                    passed(block, q, source, send_sem).wait_recv()

                    @pl.when(onward)
                    def _():
                        passed(block, q, target, send_sem).start()

                    passed(block, q, sibling, to_sibling).start()

        for other, exists, *_rest in sides(distance):

            @pl.when(exists)
            def _():
                multiply(other)

    for q in range(CHUNKS):

        @pl.when(has_right)
        def _():
            passed(place, q, right, to_right).wait_send()

        @pl.when(has_left)
        def _():
            passed(place, q, left, to_left).wait_send()

        passed(place, q, sibling, to_sibling).wait_send()

    @pl.loop(1, chips)
    def _(distance):
        for q in range(CHUNKS):
            for other, exists, source, onward, target, send_sem in sides(distance):

                @pl.when(exists)
                def _():
                    block = other * 2 + core

                    @pl.when(onward)
                    def _():
                        passed(block, q, target, send_sem).wait_send()

                    passed(block, q, sibling, to_sibling).wait_send()

    for k in range(1, seq_count):
        filter_copy(k).wait()
    own_filter.wait()


def gathered_projection(normed, weight, filters, seq_count, tensor_count):
    size, model_width = normed.shape
    width = weight.shape[2]
    parts, classes, channels, freqs = filters.shape
    rows = size * tensor_count
    blocks = pltpu.SemaphoreType.DMA((tensor_count, CHUNKS))
    return pl.pallas_call(
        functools.partial(gather_kernel, seq_count, tensor_count),
        out_shape=(
            jax.ShapeDtypeStruct((3, rows, width), jnp.bfloat16),
            jax.ShapeDtypeStruct(
                (parts, classes * seq_count, channels // seq_count, freqs), jnp.bfloat16
            ),
        ),
        in_specs=[
            pl.BlockSpec(memory_space=pltpu.VMEM),
            pl.BlockSpec(memory_space=pl.ANY),
            pl.BlockSpec(memory_space=pl.ANY),
        ],
        out_specs=[pl.BlockSpec(memory_space=pltpu.VMEM), pl.BlockSpec(memory_space=pl.ANY)],
        scratch_shapes=[
            pltpu.VMEM((tensor_count, size, model_width), jnp.bfloat16),
            pltpu.VMEM(weight.shape, jnp.bfloat16),
            pltpu.SemaphoreType.DMA,
            pltpu.SemaphoreType.DMA,
            pltpu.SemaphoreType.DMA((seq_count,)),
            pltpu.SemaphoreType.DMA((seq_count,)),
            blocks, blocks, blocks, blocks,
        ],
        compiler_params=pltpu.CompilerParams(
            vmem_limit_bytes=VMEM_LIMIT, collective_id=0, has_side_effects=True
        ),
        cost_estimate=pl.CostEstimate(
            flops=6 * rows * model_width * width, bytes_accessed=6 * model_width * width, transcendentals=0
        ),
        name="gathered_projection",
    )(normed, weight, filters)


def short_kernel(seq_count, proj_ref, carried_ref, taps_ref, queries_ref, product_ref):
    width = queries_ref.shape[1]
    piece = width // seq_count

    def branch(j, begin):
        columns = pl.ds(begin, piece)
        ext = jnp.concatenate(
            [carried_ref[j, :, columns].astype(jnp.float32), proj_ref[j, :, columns].astype(jnp.float32)],
            axis=0,
        )
        taps = taps_ref[:, j, pl.ds(begin, piece)]
        total = ext[HALO:] * taps[0:1]
        for offset in range(1, TAPS):
            total = total + pltpu.roll(ext, offset, 0)[HALO:] * taps[offset : offset + 1]
        return total

    for place in range(seq_count):
        begin = place * piece
        queries_ref[:, pl.ds(begin, piece)] = branch(0, begin)
        product_ref[place] = (branch(1, begin) * branch(2, begin)).astype(jnp.bfloat16)


def short_products(projected, carried, short_filter, seq_count):
    rows, width = projected.shape[1:]
    return pl.pallas_call(
        functools.partial(short_kernel, seq_count),
        out_shape=(
            jax.ShapeDtypeStruct((rows, width), jnp.float32),
            jax.ShapeDtypeStruct((seq_count, rows, width // seq_count), jnp.bfloat16),
        ),
        in_specs=[pl.BlockSpec(memory_space=pltpu.VMEM)] * 3,
        out_specs=[pl.BlockSpec(memory_space=pltpu.VMEM)] * 2,
        compiler_params=pltpu.CompilerParams(vmem_limit_bytes=VMEM_LIMIT),
        cost_estimate=pl.CostEstimate(
            flops=20 * rows * width, bytes_accessed=12 * rows * width, transcendentals=0
        ),
        name="short_products",
    )(projected, carried, short_filter)


def mixed(terms):
    total = None
    for weight, value in terms:
        if abs(weight) < 1e-12:
            continue
        if abs(abs(weight) - 1.0) < 1e-12:
            term = value if weight > 0 else -value
        else:
            term = value * np.float32(weight)
        total = term if total is None else total + term
    return total


def conv_kernel(
    x_ref, g_ref, cos_ref, sin_ref, turn_cos_ref, turn_sin_ref, out_ref, xt, y_real, y_imag, z_real, z_imag
):
    count, rows, piece = x_ref.shape
    classes = count + 1
    freq_count = 2 * count
    total_length = freq_count * rows
    for s in range(count):
        xt[s] = x_ref[s].astype(jnp.float32).T
    for tile in range(rows // COLUMNS):
        columns = pl.ds(tile * COLUMNS, COLUMNS)
        blocks = [xt[s, :, columns] for s in range(count)]
        for r in range(classes):
            cos_r, sin_r = turn(r, freq_count, np.arange(count))
            real = mixed([(cos_r[s], blocks[s]) for s in range(count)])
            imag = mixed([(-sin_r[s], blocks[s]) for s in range(count)])
            turn_cos = turn_cos_ref[r : r + 1, columns]
            turn_sin = turn_sin_ref[r : r + 1, columns]
            if imag is None:
                turned_real, turned_imag = real * turn_cos, -(real * turn_sin)
            else:
                turned_real = real * turn_cos + imag * turn_sin
                turned_imag = imag * turn_cos - real * turn_sin
            y_real[pl.ds(r * piece, piece), columns] = turned_real.astype(jnp.bfloat16)
            y_imag[pl.ds(r * piece, piece), columns] = turned_imag.astype(jnp.bfloat16)

    def dot(a, b):
        return jnp.dot(a, b, preferred_element_type=jnp.float32)

    @pl.loop(0, rows // COLUMNS)
    def _(tile):
        columns = pl.ds(pl.multiple_of(tile * COLUMNS, COLUMNS), COLUMNS)
        table_cos, table_sin = cos_ref[:, columns], sin_ref[:, columns]
        for r in range(classes):
            place = pl.ds(r * piece, piece)
            real_in, imag_in = y_real[place], y_imag[place]
            if r == 0:
                real = dot(real_in, table_cos)
                imag = -dot(real_in, table_sin)
            else:
                real = dot(real_in, table_cos) + dot(imag_in, table_sin)
                imag = dot(imag_in, table_cos) - dot(real_in, table_sin)
            g_real = g_ref[0, r, :, columns].astype(jnp.float32)
            g_imag = g_ref[1, r, :, columns].astype(jnp.float32)
            z_real[place, columns] = (real * g_real - imag * g_imag).astype(jnp.bfloat16)
            z_imag[place, columns] = (real * g_imag + imag * g_real).astype(jnp.bfloat16)

    @pl.loop(0, rows // COLUMNS)
    def _(tile):
        columns = pl.ds(pl.multiple_of(tile * COLUMNS, COLUMNS), COLUMNS)
        table_cos, table_sin = cos_ref[:, columns], sin_ref[:, columns]
        sums = [None] * count
        for r in range(classes):
            place = pl.ds(r * piece, piece)
            real_in, imag_in = z_real[place], z_imag[place]
            real = dot(real_in, table_cos) - dot(imag_in, table_sin)
            if r == 0:
                turned_real, turned_imag = real, None
            else:
                imag = dot(imag_in, table_cos) + dot(real_in, table_sin)
                turn_cos = turn_cos_ref[r : r + 1, columns]
                turn_sin = turn_sin_ref[r : r + 1, columns]
                turned_real = real * turn_cos - imag * turn_sin
                turned_imag = imag * turn_cos + real * turn_sin
            cos_r, sin_r = turn(r, freq_count, np.arange(count))
            for s in range(count):
                terms = [(1.0, sums[s])] if sums[s] is not None else []
                terms += [(cos_r[s], turned_real), (-sin_r[s], turned_imag)]
                sums[s] = mixed(terms)
        for s in range(count):
            out_ref[s, columns, :] = (sums[s] * np.float32(1.0 / total_length)).T.astype(jnp.bfloat16)


def long_convolution(blocks, response, tables):
    count, rows, piece = blocks.shape
    classes = count + 1
    flops = (16 * classes) * piece * rows * rows
    return pl.pallas_call(
        conv_kernel,
        out_shape=jax.ShapeDtypeStruct((count, rows, piece), jnp.bfloat16),
        in_specs=[pl.BlockSpec(memory_space=pltpu.VMEM)] * 6,
        out_specs=pl.BlockSpec(memory_space=pltpu.VMEM),
        scratch_shapes=[
            pltpu.VMEM((count, piece, rows), jnp.float32),
            pltpu.VMEM((classes * piece, rows), jnp.bfloat16),
            pltpu.VMEM((classes * piece, rows), jnp.bfloat16),
            pltpu.VMEM((classes * piece, rows), jnp.bfloat16),
            pltpu.VMEM((classes * piece, rows), jnp.bfloat16),
        ],
        compiler_params=pltpu.CompilerParams(vmem_limit_bytes=VMEM_LIMIT),
        cost_estimate=pl.CostEstimate(
            flops=flops, bytes_accessed=4 * rows * rows + 4 * classes * piece * rows, transcendentals=0
        ),
        name="long_convolution",
    )(blocks, response, *tables)


def folded_response(spectrum):
    freq_count, rows = spectrum.shape[1], spectrum.shape[3]
    half = freq_count // 2
    mirror = np.eye(rows, dtype=np.float32)[::-1]
    upper = jnp.einsum(
        "ckej,jm->ckem",
        spectrum[:, half + 1 :][:, ::-1],
        jnp.asarray(mirror, jnp.bfloat16),
        preferred_element_type=jnp.float32,
    )
    upper = upper * jnp.array([1.0, -1.0], jnp.float32)[:, None, None, None]
    middle = (spectrum[:, 1:half].astype(jnp.float32) + upper).astype(jnp.bfloat16)
    return jnp.concatenate([spectrum[:, :1], middle, spectrum[:, half : half + 1]], axis=1)


def dft_tables(rows, count):
    index = np.arange(rows)
    table_cos, table_sin = turn(index[:, None], rows, index[None, :])
    classes = np.arange(count + 1)
    turn_cos, turn_sin = turn(classes[:, None], 2 * count * rows, index[None, :])
    return (
        jnp.asarray(table_cos, jnp.bfloat16),
        jnp.asarray(table_sin, jnp.bfloat16),
        jnp.asarray(turn_cos, jnp.float32),
        jnp.asarray(turn_sin, jnp.float32),
    )


def per_device(tokens, norm_gain, in_weight, short_filter, filter_spectrum, out_weight):
    seq_count = lax.axis_size("seq")
    inputs = tokens.astype(jnp.float32)
    square_mean = jnp.mean(inputs * inputs, axis=-1, keepdims=True)
    normed = (inputs / jnp.sqrt(square_mean + EPS) * norm_gain).astype(jnp.bfloat16)
    width = in_weight.shape[2]
    projected, spectrum = gathered_projection(
        normed,
        in_weight.transpose(1, 0, 2),
        filter_spectrum.astype(jnp.bfloat16),
        seq_count,
        lax.axis_size("tensor"),
    )
    rows = projected.shape[1]
    tables = dft_tables(rows, seq_count)
    route = [(i, i + 1) for i in range(seq_count - 1)]
    carried = lax.ppermute(projected[:, rows - HALO :], "seq", route)
    response = folded_response(spectrum)
    queries, product = short_products(projected, carried, short_filter, seq_count)
    blocks = lax.all_to_all(product, "seq", split_axis=0, concat_axis=0, tiled=True)
    values = long_convolution(blocks, response, tables)
    returned = lax.all_to_all(values, "seq", split_axis=0, concat_axis=0, tiled=True)
    long_conv = returned.transpose(1, 0, 2).reshape(rows, width).astype(jnp.float32)
    gated = (queries * long_conv).astype(jnp.bfloat16)
    summed = lax.psum_scatter(
        jnp.dot(gated, out_weight, preferred_element_type=jnp.float32).astype(jnp.bfloat16),
        "tensor",
        scatter_dimension=0,
        tiled=True,
    ).astype(jnp.float32)
    return (inputs + summed).astype(jnp.bfloat16)


def solution(mesh):
    in_specs = (
        P(("seq", "tensor"), None),
        P(),
        P(None, None, "tensor"),
        P(None, None, "tensor"),
        P(None, "seq", "tensor", None),
        P("tensor", None),
    )
    out_specs = P(("seq", "tensor"), None)
    return jax.shard_map(
        per_device, mesh=mesh, in_specs=in_specs, out_specs=out_specs, check_vma=False
    )
```

```python
import functools

import jax
import jax.numpy as jnp
import numpy as np
from jax import lax
from jax.experimental import pallas as pl
from jax.experimental.pallas import tpu as pltpu
from jax.sharding import PartitionSpec as P

TAPS = 3
EPS = 1e-06
HALO = 16
COLUMNS = 256
VMEM_LIMIT = 56 * 1024 * 1024


def turn(count, total, index):
    angle = 2.0 * np.pi * ((np.asarray(count) * np.asarray(index)) % total) / total
    return np.cos(angle), np.sin(angle)


MESH = pl.DeviceIdType.MESH
CHUNKS = 4


def gather_kernel(
    seq_count, tensor_count, normed_ref, weight_ref, filter_ref, proj_ref, spectrum_ref,
    held, weights, weight_sem, own_sem, filter_send, filter_recv, recv, to_right, to_left, to_sibling,
):
    seq_place = lax.axis_index("seq")
    place = lax.axis_index("tensor")
    chips = tensor_count // 2
    chip, core = place // 2, place % 2
    sibling = chip * 2 + 1 - core
    has_right, has_left = chip < chips - 1, chip > 0
    right, left = place + 2, place - 2
    size = held.shape[1]
    step = size // CHUNKS
    classes = filter_ref.shape[1]
    piece = spectrum_ref.shape[2]
    width = weight_ref.shape[2]

    weight_copy = pltpu.make_async_copy(weight_ref, weights, weight_sem)
    weight_copy.start()
    own_filter = pltpu.make_async_copy(
        filter_ref.at[:, :, pl.ds(seq_place * piece, piece), :],
        spectrum_ref.at[:, pl.ds(seq_place * classes, classes), :, :],
        own_sem,
    )
    own_filter.start()
    held[place] = normed_ref[...]

    barrier = pltpu.get_barrier_semaphore()
    pl.semaphore_signal(barrier, inc=1, device_id={"tensor": sibling}, device_id_type=MESH)

    @pl.when(has_right)
    def _():
        pl.semaphore_signal(barrier, inc=1, device_id={"tensor": right}, device_id_type=MESH)

    @pl.when(has_left)
    def _():
        pl.semaphore_signal(barrier, inc=1, device_id={"tensor": left}, device_id_type=MESH)

    for k in range(1, seq_count):
        peer = lax.rem(seq_place + k, seq_count)
        pl.semaphore_signal(barrier, inc=1, device_id={"seq": peer}, device_id_type=MESH)
    neighbours = has_right.astype(jnp.int32) + has_left.astype(jnp.int32)
    pl.semaphore_wait(barrier, seq_count + neighbours)

    def passed(block, q, target, send_sem):
        part = held.at[block, pl.ds(q * step, step)]
        return pltpu.make_async_remote_copy(
            src_ref=part,
            dst_ref=part,
            send_sem=send_sem.at[block, q],
            recv_sem=recv.at[block, q],
            device_id={"tensor": target},
            device_id_type=MESH,
        )

    def filter_copy(k):
        peer = lax.rem(seq_place + k, seq_count)
        return pltpu.make_async_remote_copy(
            src_ref=filter_ref.at[:, :, pl.ds(peer * piece, piece), :],
            dst_ref=spectrum_ref.at[:, pl.ds(seq_place * classes, classes), :, :],
            send_sem=filter_send.at[k],
            recv_sem=filter_recv.at[k],
            device_id={"seq": peer},
            device_id_type=MESH,
        )

    def multiply(other):
        for q in range(CHUNKS):
            passed(other * 2 + 1 - core, q, sibling, to_sibling).wait_recv()
        rows = pl.ds(pl.multiple_of(other * 2 * size, 2 * size), 2 * size)

        @pl.loop(0, 3)
        def _(j):
            for begin in range(0, width, 256):
                columns = min(256, width - begin)
                value = jnp.dot(
                    held[pl.ds(other * 2, 2)].reshape(2 * size, held.shape[2]),
                    weights[j, :, pl.ds(begin, columns)],
                    preferred_element_type=jnp.float32,
                )
                proj_ref[j, rows, pl.ds(begin, columns)] = value.astype(jnp.bfloat16)

    for q in range(CHUNKS):

        @pl.when(has_right)
        def _():
            passed(place, q, right, to_right).start()

        @pl.when(has_left)
        def _():
            passed(place, q, left, to_left).start()

        passed(place, q, sibling, to_sibling).start()
    for k in range(1, seq_count):
        filter_copy(k).start()
    weight_copy.wait()
    multiply(chip)

    def sides(distance):
        yield chip + distance, chip + distance < chips, right, has_left, left, to_left
        yield chip - distance, chip - distance >= 0, left, has_right, right, to_right

    @pl.loop(1, chips)
    def _(distance):
        for q in range(CHUNKS):
            for other, exists, source, onward, target, send_sem in sides(distance):

                @pl.when(exists)
                def _():
                    block = other * 2 + core
                    passed(block, q, source, send_sem).wait_recv()

                    @pl.when(onward)
                    def _():
                        passed(block, q, target, send_sem).start()

                    passed(block, q, sibling, to_sibling).start()

        for other, exists, *_rest in sides(distance):

            @pl.when(exists)
            def _():
                multiply(other)

    for q in range(CHUNKS):

        @pl.when(has_right)
        def _():
            passed(place, q, right, to_right).wait_send()

        @pl.when(has_left)
        def _():
            passed(place, q, left, to_left).wait_send()

        passed(place, q, sibling, to_sibling).wait_send()

    @pl.loop(1, chips)
    def _(distance):
        for q in range(CHUNKS):
            for other, exists, source, onward, target, send_sem in sides(distance):

                @pl.when(exists)
                def _():
                    block = other * 2 + core

                    @pl.when(onward)
                    def _():
                        passed(block, q, target, send_sem).wait_send()

                    passed(block, q, sibling, to_sibling).wait_send()

    for k in range(1, seq_count):
        filter_copy(k).wait()
    own_filter.wait()


def gathered_projection(normed, weight, filters, seq_count, tensor_count):
    size, model_width = normed.shape
    width = weight.shape[2]
    parts, classes, channels, freqs = filters.shape
    rows = size * tensor_count
    blocks = pltpu.SemaphoreType.DMA((tensor_count, CHUNKS))
    return pl.pallas_call(
        functools.partial(gather_kernel, seq_count, tensor_count),
        out_shape=(
            jax.ShapeDtypeStruct((3, rows, width), jnp.bfloat16),
            jax.ShapeDtypeStruct(
                (parts, classes * seq_count, channels // seq_count, freqs), jnp.bfloat16
            ),
        ),
        in_specs=[
            pl.BlockSpec(memory_space=pltpu.VMEM),
            pl.BlockSpec(memory_space=pl.ANY),
            pl.BlockSpec(memory_space=pl.ANY),
        ],
        out_specs=[pl.BlockSpec(memory_space=pltpu.VMEM), pl.BlockSpec(memory_space=pl.ANY)],
        scratch_shapes=[
            pltpu.VMEM((tensor_count, size, model_width), jnp.bfloat16),
            pltpu.VMEM(weight.shape, jnp.bfloat16),
            pltpu.SemaphoreType.DMA,
            pltpu.SemaphoreType.DMA,
            pltpu.SemaphoreType.DMA((seq_count,)),
            pltpu.SemaphoreType.DMA((seq_count,)),
            blocks, blocks, blocks, blocks,
        ],
        compiler_params=pltpu.CompilerParams(
            vmem_limit_bytes=VMEM_LIMIT, collective_id=0, has_side_effects=True
        ),
        cost_estimate=pl.CostEstimate(
            flops=6 * rows * model_width * width, bytes_accessed=6 * model_width * width, transcendentals=0
        ),
        name="gathered_projection",
    )(normed, weight, filters)


def scatter_kernel(
    tensor_count, tokens_ref, queries_ref, values_ref, own_ref, other_ref, out_ref,
    gated, shared, outgoing, from_left, from_right, totals,
    share_send, share_recv, send_right, send_left, recv_left, recv_right,
):
    place = lax.axis_index("tensor")
    chips = tensor_count // 2
    chip, core = place // 2, place % 2
    sibling = chip * 2 + 1 - core
    has_right, has_left = chip < chips - 1, chip > 0
    right, left = place + 2, place - 2
    size, model_width = tokens_ref.shape
    step = model_width // CHUNKS
    count, rows, piece = values_ref.shape

    barrier = pltpu.get_barrier_semaphore()
    pl.semaphore_signal(barrier, inc=1, device_id={"tensor": sibling}, device_id_type=MESH)

    @pl.when(has_right)
    def _():
        pl.semaphore_signal(barrier, inc=1, device_id={"tensor": right}, device_id_type=MESH)

    @pl.when(has_left)
    def _():
        pl.semaphore_signal(barrier, inc=1, device_id={"tensor": left}, device_id_type=MESH)

    for s in range(count):
        columns = pl.ds(s * piece, piece)
        value = queries_ref[:, columns] * values_ref[s].astype(jnp.float32)
        gated[:, :, :, columns] = value.astype(jnp.bfloat16).reshape(chips, 2, size, piece)

    neighbours = has_right.astype(jnp.int32) + has_left.astype(jnp.int32)
    pl.semaphore_wait(barrier, 1 + neighbours)
    share = pltpu.make_async_remote_copy(
        src_ref=gated.at[:, 1 - core],
        dst_ref=shared,
        send_sem=share_send,
        recv_sem=share_recv,
        device_id={"tensor": sibling},
        device_id_type=MESH,
    )
    share.start()
    share.wait()

    def rightward(dest, q):
        columns = pl.ds(q * step, step)
        return pltpu.make_async_remote_copy(
            src_ref=outgoing.at[dest, :, columns],
            dst_ref=from_left.at[dest, :, columns],
            send_sem=send_right.at[dest, q],
            recv_sem=recv_left.at[dest, q],
            device_id={"tensor": right},
            device_id_type=MESH,
        )

    def leftward(dest, q):
        columns = pl.ds(q * step, step)
        return pltpu.make_async_remote_copy(
            src_ref=outgoing.at[dest, :, columns],
            dst_ref=from_right.at[dest, :, columns],
            send_sem=send_left.at[dest, q],
            recv_sem=recv_right.at[dest, q],
            device_id={"tensor": left},
            device_id_type=MESH,
        )

    def partial(dest, columns):
        return jnp.dot(
            gated[dest, core], own_ref[:, columns], preferred_element_type=jnp.float32
        ) + jnp.dot(shared[dest], other_ref[:, columns], preferred_element_type=jnp.float32)

    def tiles(q):
        width = min(512, step)
        for begin in range(0, step, width):
            yield pl.ds(q * step + begin, width)

    def relay(dest, q, has_more, arriving, buffer):
        for columns in tiles(q):
            outgoing[dest, :, columns] = partial(dest, columns).astype(jnp.bfloat16)

        @pl.when(has_more)
        def _():
            arriving(dest, q).wait_recv()
            for columns in tiles(q):
                total = outgoing[dest, :, columns].astype(jnp.float32) + buffer[
                    dest, :, columns
                ].astype(jnp.float32)
                outgoing[dest, :, columns] = total.astype(jnp.bfloat16)

    @pl.loop(0, chips - 1)
    def _(i):
        for q in range(CHUNKS):
            far = chips - 1 - i

            @pl.when(far > chip)
            def _():
                relay(far, q, has_left, rightward, from_left)
                rightward(far, q).start()

            @pl.when(i < chip)
            def _():
                relay(i, q, has_right, leftward, from_right)
                leftward(i, q).start()

    for q in range(CHUNKS):
        for columns in tiles(q):
            totals[:, columns] = tokens_ref[:, columns].astype(jnp.float32) + partial(chip, columns)
    for q in range(CHUNKS):

        @pl.when(has_left)
        def _():
            rightward(chip, q).wait_recv()
            for columns in tiles(q):
                totals[:, columns] += from_left[chip, :, columns].astype(jnp.float32)

        @pl.when(has_right)
        def _():
            leftward(chip, q).wait_recv()
            for columns in tiles(q):
                totals[:, columns] += from_right[chip, :, columns].astype(jnp.float32)

        for columns in tiles(q):
            out_ref[:, columns] = totals[:, columns].astype(jnp.bfloat16)

    @pl.loop(0, chips - 1)
    def _(i):
        for q in range(CHUNKS):
            far = chips - 1 - i

            @pl.when(far > chip)
            def _():
                rightward(far, q).wait_send()

            @pl.when(i < chip)
            def _():
                leftward(i, q).wait_send()


def scattered_output(tokens, queries, values, own_weight, other_weight, tensor_count):
    size, model_width = tokens.shape
    rows, width = queries.shape
    chips = tensor_count // 2
    line = pltpu.VMEM((chips, size, model_width), jnp.bfloat16)
    flags = pltpu.SemaphoreType.DMA((chips, CHUNKS))
    return pl.pallas_call(
        functools.partial(scatter_kernel, tensor_count),
        out_shape=jax.ShapeDtypeStruct((size, model_width), jnp.bfloat16),
        in_specs=[pl.BlockSpec(memory_space=pltpu.VMEM)] * 5,
        out_specs=pl.BlockSpec(memory_space=pltpu.VMEM),
        scratch_shapes=[
            pltpu.VMEM((chips, 2, size, width), jnp.bfloat16),
            pltpu.VMEM((chips, size, width), jnp.bfloat16),
            line, line, line,
            pltpu.VMEM((size, model_width), jnp.float32),
            pltpu.SemaphoreType.DMA,
            pltpu.SemaphoreType.DMA,
            flags, flags, flags, flags,
        ],
        compiler_params=pltpu.CompilerParams(
            vmem_limit_bytes=VMEM_LIMIT, collective_id=1, has_side_effects=True
        ),
        cost_estimate=pl.CostEstimate(
            flops=2 * rows * model_width * width, bytes_accessed=4 * model_width * width, transcendentals=0
        ),
        name="scattered_output",
    )(tokens, queries, values, own_weight, other_weight)


def short_kernel(seq_count, proj_ref, carried_ref, taps_ref, queries_ref, product_ref):
    width = queries_ref.shape[1]
    piece = width // seq_count

    def branch(j, begin):
        columns = pl.ds(begin, piece)
        ext = jnp.concatenate(
            [carried_ref[j, :, columns].astype(jnp.float32), proj_ref[j, :, columns].astype(jnp.float32)],
            axis=0,
        )
        taps = taps_ref[:, j, pl.ds(begin, piece)]
        total = ext[HALO:] * taps[0:1]
        for offset in range(1, TAPS):
            total = total + pltpu.roll(ext, offset, 0)[HALO:] * taps[offset : offset + 1]
        return total

    for place in range(seq_count):
        begin = place * piece
        queries_ref[:, pl.ds(begin, piece)] = branch(0, begin)
        product_ref[place] = (branch(1, begin) * branch(2, begin)).astype(jnp.bfloat16)


def short_products(projected, carried, short_filter, seq_count):
    rows, width = projected.shape[1:]
    return pl.pallas_call(
        functools.partial(short_kernel, seq_count),
        out_shape=(
            jax.ShapeDtypeStruct((rows, width), jnp.float32),
            jax.ShapeDtypeStruct((seq_count, rows, width // seq_count), jnp.bfloat16),
        ),
        in_specs=[pl.BlockSpec(memory_space=pltpu.VMEM)] * 3,
        out_specs=[pl.BlockSpec(memory_space=pltpu.VMEM)] * 2,
        compiler_params=pltpu.CompilerParams(vmem_limit_bytes=VMEM_LIMIT),
        cost_estimate=pl.CostEstimate(
            flops=20 * rows * width, bytes_accessed=12 * rows * width, transcendentals=0
        ),
        name="short_products",
    )(projected, carried, short_filter)


def mixed(terms):
    total = None
    for weight, value in terms:
        if abs(weight) < 1e-12:
            continue
        if abs(abs(weight) - 1.0) < 1e-12:
            term = value if weight > 0 else -value
        else:
            term = value * np.float32(weight)
        total = term if total is None else total + term
    return total


def conv_kernel(
    x_ref, g_ref, cos_ref, sin_ref, turn_cos_ref, turn_sin_ref, out_ref, xt, y_real, y_imag, z_real, z_imag
):
    count, rows, piece = x_ref.shape
    classes = count + 1
    freq_count = 2 * count
    total_length = freq_count * rows
    for s in range(count):
        xt[s] = x_ref[s].astype(jnp.float32).T
    for tile in range(rows // COLUMNS):
        columns = pl.ds(tile * COLUMNS, COLUMNS)
        blocks = [xt[s, :, columns] for s in range(count)]
        for r in range(classes):
            cos_r, sin_r = turn(r, freq_count, np.arange(count))
            real = mixed([(cos_r[s], blocks[s]) for s in range(count)])
            imag = mixed([(-sin_r[s], blocks[s]) for s in range(count)])
            turn_cos = turn_cos_ref[r : r + 1, columns]
            turn_sin = turn_sin_ref[r : r + 1, columns]
            if imag is None:
                turned_real, turned_imag = real * turn_cos, -(real * turn_sin)
            else:
                turned_real = real * turn_cos + imag * turn_sin
                turned_imag = imag * turn_cos - real * turn_sin
            y_real[pl.ds(r * piece, piece), columns] = turned_real.astype(jnp.bfloat16)
            y_imag[pl.ds(r * piece, piece), columns] = turned_imag.astype(jnp.bfloat16)

    def dot(a, b):
        return jnp.dot(a, b, preferred_element_type=jnp.float32)

    @pl.loop(0, rows // COLUMNS)
    def _(tile):
        columns = pl.ds(pl.multiple_of(tile * COLUMNS, COLUMNS), COLUMNS)
        table_cos, table_sin = cos_ref[:, columns], sin_ref[:, columns]
        for r in range(classes):
            place = pl.ds(r * piece, piece)
            real_in, imag_in = y_real[place], y_imag[place]
            if r == 0:
                real = dot(real_in, table_cos)
                imag = -dot(real_in, table_sin)
            else:
                real = dot(real_in, table_cos) + dot(imag_in, table_sin)
                imag = dot(imag_in, table_cos) - dot(real_in, table_sin)
            g_real = g_ref[0, r, :, columns].astype(jnp.float32)
            g_imag = g_ref[1, r, :, columns].astype(jnp.float32)
            z_real[place, columns] = (real * g_real - imag * g_imag).astype(jnp.bfloat16)
            z_imag[place, columns] = (real * g_imag + imag * g_real).astype(jnp.bfloat16)

    @pl.loop(0, rows // COLUMNS)
    def _(tile):
        columns = pl.ds(pl.multiple_of(tile * COLUMNS, COLUMNS), COLUMNS)
        table_cos, table_sin = cos_ref[:, columns], sin_ref[:, columns]
        sums = [None] * count
        for r in range(classes):
            place = pl.ds(r * piece, piece)
            real_in, imag_in = z_real[place], z_imag[place]
            real = dot(real_in, table_cos) - dot(imag_in, table_sin)
            if r == 0:
                turned_real, turned_imag = real, None
            else:
                imag = dot(imag_in, table_cos) + dot(real_in, table_sin)
                turn_cos = turn_cos_ref[r : r + 1, columns]
                turn_sin = turn_sin_ref[r : r + 1, columns]
                turned_real = real * turn_cos - imag * turn_sin
                turned_imag = imag * turn_cos + real * turn_sin
            cos_r, sin_r = turn(r, freq_count, np.arange(count))
            for s in range(count):
                terms = [(1.0, sums[s])] if sums[s] is not None else []
                terms += [(cos_r[s], turned_real), (-sin_r[s], turned_imag)]
                sums[s] = mixed(terms)
        for s in range(count):
            out_ref[s, columns, :] = (sums[s] * np.float32(1.0 / total_length)).T.astype(jnp.bfloat16)


def long_convolution(blocks, response, tables):
    count, rows, piece = blocks.shape
    classes = count + 1
    flops = (16 * classes) * piece * rows * rows
    return pl.pallas_call(
        conv_kernel,
        out_shape=jax.ShapeDtypeStruct((count, rows, piece), jnp.bfloat16),
        in_specs=[pl.BlockSpec(memory_space=pltpu.VMEM)] * 6,
        out_specs=pl.BlockSpec(memory_space=pltpu.VMEM),
        scratch_shapes=[
            pltpu.VMEM((count, piece, rows), jnp.float32),
            pltpu.VMEM((classes * piece, rows), jnp.bfloat16),
            pltpu.VMEM((classes * piece, rows), jnp.bfloat16),
            pltpu.VMEM((classes * piece, rows), jnp.bfloat16),
            pltpu.VMEM((classes * piece, rows), jnp.bfloat16),
        ],
        compiler_params=pltpu.CompilerParams(vmem_limit_bytes=VMEM_LIMIT),
        cost_estimate=pl.CostEstimate(
            flops=flops, bytes_accessed=4 * rows * rows + 4 * classes * piece * rows, transcendentals=0
        ),
        name="long_convolution",
    )(blocks, response, *tables)


def folded_response(spectrum):
    freq_count, rows = spectrum.shape[1], spectrum.shape[3]
    half = freq_count // 2
    mirror = np.eye(rows, dtype=np.float32)[::-1]
    upper = jnp.einsum(
        "ckej,jm->ckem",
        spectrum[:, half + 1 :][:, ::-1],
        jnp.asarray(mirror, jnp.bfloat16),
        preferred_element_type=jnp.float32,
    )
    upper = upper * jnp.array([1.0, -1.0], jnp.float32)[:, None, None, None]
    middle = (spectrum[:, 1:half].astype(jnp.float32) + upper).astype(jnp.bfloat16)
    return jnp.concatenate([spectrum[:, :1], middle, spectrum[:, half : half + 1]], axis=1)


def dft_tables(rows, count):
    index = np.arange(rows)
    table_cos, table_sin = turn(index[:, None], rows, index[None, :])
    classes = np.arange(count + 1)
    turn_cos, turn_sin = turn(classes[:, None], 2 * count * rows, index[None, :])
    return (
        jnp.asarray(table_cos, jnp.bfloat16),
        jnp.asarray(table_sin, jnp.bfloat16),
        jnp.asarray(turn_cos, jnp.float32),
        jnp.asarray(turn_sin, jnp.float32),
    )


def per_device(tokens, norm_gain, in_weight, short_filter, filter_spectrum, out_weight):
    seq_count = lax.axis_size("seq")
    tensor_count = lax.axis_size("tensor")
    swap = [(i, i + 1 - 2 * (i % 2)) for i in range(tensor_count)]
    other_weight = lax.ppermute(out_weight, "tensor", swap)
    inputs = tokens.astype(jnp.float32)
    square_mean = jnp.mean(inputs * inputs, axis=-1, keepdims=True)
    normed = (inputs / jnp.sqrt(square_mean + EPS) * norm_gain).astype(jnp.bfloat16)
    width = in_weight.shape[2]
    projected, spectrum = gathered_projection(
        normed,
        in_weight.transpose(1, 0, 2),
        filter_spectrum.astype(jnp.bfloat16),
        seq_count,
        tensor_count,
    )
    rows = projected.shape[1]
    tables = dft_tables(rows, seq_count)
    route = [(i, i + 1) for i in range(seq_count - 1)]
    carried = lax.ppermute(projected[:, rows - HALO :], "seq", route)
    response = folded_response(spectrum)
    queries, product = short_products(projected, carried, short_filter, seq_count)
    blocks = lax.all_to_all(product, "seq", split_axis=0, concat_axis=0, tiled=True)
    values = long_convolution(blocks, response, tables)
    returned = lax.all_to_all(values, "seq", split_axis=0, concat_axis=0, tiled=True)
    return scattered_output(tokens, queries, returned, out_weight, other_weight, tensor_count)


def solution(mesh):
    in_specs = (
        P(("seq", "tensor"), None),
        P(),
        P(None, None, "tensor"),
        P(None, None, "tensor"),
        P(None, "seq", "tensor", None),
        P("tensor", None),
    )
    out_specs = P(("seq", "tensor"), None)
    return jax.shard_map(
        per_device, mesh=mesh, in_specs=in_specs, out_specs=out_specs, check_vma=False
    )
```

```python
import functools

import jax
import jax.numpy as jnp
import numpy as np
from jax import lax
from jax.experimental import pallas as pl
from jax.experimental.pallas import tpu as pltpu
from jax.sharding import PartitionSpec as P

TAPS = 3
EPS = 1e-06
HALO = 16
COLUMNS = 256
VMEM_LIMIT = 56 * 1024 * 1024


def turn(count, total, index):
    angle = 2.0 * np.pi * ((np.asarray(count) * np.asarray(index)) % total) / total
    return np.cos(angle), np.sin(angle)


MESH = pl.DeviceIdType.MESH
CHUNKS = 4


def gather_kernel(
    seq_count, tensor_count, normed_ref, weight_ref, filter_ref, proj_ref, spectrum_ref,
    held, weights, weight_sem, own_sem, filter_send, filter_recv, recv, to_right, to_left, to_sibling,
):
    seq_place = lax.axis_index("seq")
    place = lax.axis_index("tensor")
    chips = tensor_count // 2
    chip, core = place // 2, place % 2
    sibling = chip * 2 + 1 - core
    has_right, has_left = chip < chips - 1, chip > 0
    right, left = place + 2, place - 2
    size = held.shape[1]
    step = size // CHUNKS
    classes = filter_ref.shape[1]
    piece = spectrum_ref.shape[2]
    width = weight_ref.shape[2]

    weight_copy = pltpu.make_async_copy(weight_ref, weights, weight_sem)
    weight_copy.start()
    own_filter = pltpu.make_async_copy(
        filter_ref.at[:, :, pl.ds(seq_place * piece, piece), :],
        spectrum_ref.at[:, pl.ds(seq_place * classes, classes), :, :],
        own_sem,
    )
    own_filter.start()
    held[place] = normed_ref[...]

    barrier = pltpu.get_barrier_semaphore()
    pl.semaphore_signal(barrier, inc=1, device_id={"tensor": sibling}, device_id_type=MESH)

    @pl.when(has_right)
    def _():
        pl.semaphore_signal(barrier, inc=1, device_id={"tensor": right}, device_id_type=MESH)

    @pl.when(has_left)
    def _():
        pl.semaphore_signal(barrier, inc=1, device_id={"tensor": left}, device_id_type=MESH)

    for k in range(1, seq_count):
        peer = lax.rem(seq_place + k, seq_count)
        pl.semaphore_signal(barrier, inc=1, device_id={"seq": peer}, device_id_type=MESH)
    neighbours = has_right.astype(jnp.int32) + has_left.astype(jnp.int32)
    pl.semaphore_wait(barrier, seq_count + neighbours)

    def passed(block, q, target, send_sem):
        part = held.at[block, pl.ds(q * step, step)]
        return pltpu.make_async_remote_copy(
            src_ref=part,
            dst_ref=part,
            send_sem=send_sem.at[block, q],
            recv_sem=recv.at[block, q],
            device_id={"tensor": target},
            device_id_type=MESH,
        )

    def filter_copy(k):
        peer = lax.rem(seq_place + k, seq_count)
        return pltpu.make_async_remote_copy(
            src_ref=filter_ref.at[:, :, pl.ds(peer * piece, piece), :],
            dst_ref=spectrum_ref.at[:, pl.ds(seq_place * classes, classes), :, :],
            send_sem=filter_send.at[k],
            recv_sem=filter_recv.at[k],
            device_id={"seq": peer},
            device_id_type=MESH,
        )

    def multiply(other, j):
        if j == 0:
            for q in range(CHUNKS):
                passed(other * 2 + 1 - core, q, sibling, to_sibling).wait_recv()
        rows = pl.ds(pl.multiple_of(other * 2 * size, 2 * size), 2 * size)
        for begin in range(0, width, 256):
            columns = min(256, width - begin)
            value = jnp.dot(
                held[pl.ds(other * 2, 2)].reshape(2 * size, held.shape[2]),
                weights[j, :, pl.ds(begin, columns)],
                preferred_element_type=jnp.float32,
            )
            proj_ref[j, rows, pl.ds(begin, columns)] = value.astype(jnp.bfloat16)

    for q in range(CHUNKS):

        @pl.when(has_right)
        def _():
            passed(place, q, right, to_right).start()

        @pl.when(has_left)
        def _():
            passed(place, q, left, to_left).start()

        passed(place, q, sibling, to_sibling).start()
    for k in range(1, seq_count):
        filter_copy(k).start()
    weight_copy.wait()

    def sides(distance):
        yield chip + distance, chip + distance < chips, right, has_left, left, to_left
        yield chip - distance, chip - distance >= 0, left, has_right, right, to_right

    @pl.loop(1, chips)
    def _(distance):
        for q in range(CHUNKS):
            for other, exists, source, onward, target, send_sem in sides(distance):

                @pl.when(exists)
                def _():
                    block = other * 2 + core
                    passed(block, q, source, send_sem).wait_recv()

                    @pl.when(onward)
                    def _():
                        passed(block, q, target, send_sem).start()

                    passed(block, q, sibling, to_sibling).start()

            if q < 3:
                for side, (other, exists, *_rest) in enumerate(sides(distance - 1)):

                    @pl.when(exists & (distance > side))
                    def _():
                        multiply(other, q)

    for other, exists, *_rest in sides(chips - 1):

        @pl.when(exists)
        def _():
            for j in range(3):
                multiply(other, j)

    for q in range(CHUNKS):

        @pl.when(has_right)
        def _():
            passed(place, q, right, to_right).wait_send()

        @pl.when(has_left)
        def _():
            passed(place, q, left, to_left).wait_send()

        passed(place, q, sibling, to_sibling).wait_send()

    @pl.loop(1, chips)
    def _(distance):
        for q in range(CHUNKS):
            for other, exists, source, onward, target, send_sem in sides(distance):

                @pl.when(exists)
                def _():
                    block = other * 2 + core

                    @pl.when(onward)
                    def _():
                        passed(block, q, target, send_sem).wait_send()

                    passed(block, q, sibling, to_sibling).wait_send()

    for k in range(1, seq_count):
        filter_copy(k).wait()
    own_filter.wait()


def gathered_projection(normed, weight, filters, seq_count, tensor_count):
    size, model_width = normed.shape
    width = weight.shape[2]
    parts, classes, channels, freqs = filters.shape
    rows = size * tensor_count
    blocks = pltpu.SemaphoreType.DMA((tensor_count, CHUNKS))
    return pl.pallas_call(
        functools.partial(gather_kernel, seq_count, tensor_count),
        out_shape=(
            jax.ShapeDtypeStruct((3, rows, width), jnp.bfloat16),
            jax.ShapeDtypeStruct(
                (parts, classes * seq_count, channels // seq_count, freqs), jnp.bfloat16
            ),
        ),
        in_specs=[
            pl.BlockSpec(memory_space=pltpu.VMEM),
            pl.BlockSpec(memory_space=pl.ANY),
            pl.BlockSpec(memory_space=pl.ANY),
        ],
        out_specs=[pl.BlockSpec(memory_space=pltpu.VMEM), pl.BlockSpec(memory_space=pl.ANY)],
        scratch_shapes=[
            pltpu.VMEM((tensor_count, size, model_width), jnp.bfloat16),
            pltpu.VMEM(weight.shape, jnp.bfloat16),
            pltpu.SemaphoreType.DMA,
            pltpu.SemaphoreType.DMA,
            pltpu.SemaphoreType.DMA((seq_count,)),
            pltpu.SemaphoreType.DMA((seq_count,)),
            blocks, blocks, blocks, blocks,
        ],
        compiler_params=pltpu.CompilerParams(
            vmem_limit_bytes=VMEM_LIMIT, collective_id=0, has_side_effects=True
        ),
        cost_estimate=pl.CostEstimate(
            flops=6 * rows * model_width * width, bytes_accessed=6 * model_width * width, transcendentals=0
        ),
        name="gathered_projection",
    )(normed, weight, filters)


def scatter_kernel(
    tensor_count, tokens_ref, queries_ref, values_ref, own_ref, other_ref, out_ref,
    gated, shared, outgoing, from_left, from_right, totals,
    share_send, share_recv, send_right, send_left, recv_left, recv_right,
):
    place = lax.axis_index("tensor")
    chips = tensor_count // 2
    chip, core = place // 2, place % 2
    sibling = chip * 2 + 1 - core
    has_right, has_left = chip < chips - 1, chip > 0
    right, left = place + 2, place - 2
    size, model_width = tokens_ref.shape
    step = model_width // CHUNKS
    count, rows, piece = values_ref.shape

    barrier = pltpu.get_barrier_semaphore()
    pl.semaphore_signal(barrier, inc=1, device_id={"tensor": sibling}, device_id_type=MESH)

    @pl.when(has_right)
    def _():
        pl.semaphore_signal(barrier, inc=1, device_id={"tensor": right}, device_id_type=MESH)

    @pl.when(has_left)
    def _():
        pl.semaphore_signal(barrier, inc=1, device_id={"tensor": left}, device_id_type=MESH)

    for s in range(count):
        columns = pl.ds(s * piece, piece)
        value = queries_ref[:, columns] * values_ref[s].astype(jnp.float32)
        gated[:, :, :, columns] = value.astype(jnp.bfloat16).reshape(chips, 2, size, piece)

    neighbours = has_right.astype(jnp.int32) + has_left.astype(jnp.int32)
    pl.semaphore_wait(barrier, 1 + neighbours)
    share = pltpu.make_async_remote_copy(
        src_ref=gated.at[:, 1 - core],
        dst_ref=shared,
        send_sem=share_send,
        recv_sem=share_recv,
        device_id={"tensor": sibling},
        device_id_type=MESH,
    )
    share.start()
    share.wait()

    def rightward(dest, q):
        columns = pl.ds(q * step, step)
        return pltpu.make_async_remote_copy(
            src_ref=outgoing.at[dest, :, columns],
            dst_ref=from_left.at[dest, :, columns],
            send_sem=send_right.at[dest, q],
            recv_sem=recv_left.at[dest, q],
            device_id={"tensor": right},
            device_id_type=MESH,
        )

    def leftward(dest, q):
        columns = pl.ds(q * step, step)
        return pltpu.make_async_remote_copy(
            src_ref=outgoing.at[dest, :, columns],
            dst_ref=from_right.at[dest, :, columns],
            send_sem=send_left.at[dest, q],
            recv_sem=recv_right.at[dest, q],
            device_id={"tensor": left},
            device_id_type=MESH,
        )

    def partial(dest, columns):
        return jnp.dot(
            gated[dest, core], own_ref[:, columns], preferred_element_type=jnp.float32
        ) + jnp.dot(shared[dest], other_ref[:, columns], preferred_element_type=jnp.float32)

    def tiles(q):
        width = min(512, step)
        for begin in range(0, step, width):
            yield pl.ds(q * step + begin, width)

    def relay(dest, q, has_more, arriving, buffer):
        for columns in tiles(q):
            outgoing[dest, :, columns] = partial(dest, columns).astype(jnp.bfloat16)

        @pl.when(has_more)
        def _():
            arriving(dest, q).wait_recv()
            for columns in tiles(q):
                total = outgoing[dest, :, columns].astype(jnp.float32) + buffer[
                    dest, :, columns
                ].astype(jnp.float32)
                outgoing[dest, :, columns] = total.astype(jnp.bfloat16)

    @pl.loop(0, chips - 1)
    def _(i):
        for q in range(CHUNKS):
            far = chips - 1 - i

            @pl.when(far > chip)
            def _():
                relay(far, q, has_left, rightward, from_left)
                rightward(far, q).start()

            @pl.when(i < chip)
            def _():
                relay(i, q, has_right, leftward, from_right)
                leftward(i, q).start()

    for q in range(CHUNKS):
        for columns in tiles(q):
            totals[:, columns] = tokens_ref[:, columns].astype(jnp.float32) + partial(chip, columns)
    for q in range(CHUNKS):

        @pl.when(has_left)
        def _():
            rightward(chip, q).wait_recv()
            for columns in tiles(q):
                totals[:, columns] += from_left[chip, :, columns].astype(jnp.float32)

        @pl.when(has_right)
        def _():
            leftward(chip, q).wait_recv()
            for columns in tiles(q):
                totals[:, columns] += from_right[chip, :, columns].astype(jnp.float32)

        for columns in tiles(q):
            out_ref[:, columns] = totals[:, columns].astype(jnp.bfloat16)

    @pl.loop(0, chips - 1)
    def _(i):
        for q in range(CHUNKS):
            far = chips - 1 - i

            @pl.when(far > chip)
            def _():
                rightward(far, q).wait_send()

            @pl.when(i < chip)
            def _():
                leftward(i, q).wait_send()


def scattered_output(tokens, queries, values, own_weight, other_weight, tensor_count):
    size, model_width = tokens.shape
    rows, width = queries.shape
    chips = tensor_count // 2
    line = pltpu.VMEM((chips, size, model_width), jnp.bfloat16)
    flags = pltpu.SemaphoreType.DMA((chips, CHUNKS))
    return pl.pallas_call(
        functools.partial(scatter_kernel, tensor_count),
        out_shape=jax.ShapeDtypeStruct((size, model_width), jnp.bfloat16),
        in_specs=[pl.BlockSpec(memory_space=pltpu.VMEM)] * 5,
        out_specs=pl.BlockSpec(memory_space=pltpu.VMEM),
        scratch_shapes=[
            pltpu.VMEM((chips, 2, size, width), jnp.bfloat16),
            pltpu.VMEM((chips, size, width), jnp.bfloat16),
            line, line, line,
            pltpu.VMEM((size, model_width), jnp.float32),
            pltpu.SemaphoreType.DMA,
            pltpu.SemaphoreType.DMA,
            flags, flags, flags, flags,
        ],
        compiler_params=pltpu.CompilerParams(
            vmem_limit_bytes=VMEM_LIMIT, collective_id=1, has_side_effects=True
        ),
        cost_estimate=pl.CostEstimate(
            flops=2 * rows * model_width * width, bytes_accessed=4 * model_width * width, transcendentals=0
        ),
        name="scattered_output",
    )(tokens, queries, values, own_weight, other_weight)


def short_kernel(seq_count, proj_ref, carried_ref, taps_ref, queries_ref, product_ref):
    width = queries_ref.shape[1]
    piece = width // seq_count

    def branch(j, begin):
        columns = pl.ds(begin, piece)
        ext = jnp.concatenate(
            [carried_ref[j, :, columns].astype(jnp.float32), proj_ref[j, :, columns].astype(jnp.float32)],
            axis=0,
        )
        taps = taps_ref[:, j, pl.ds(begin, piece)]
        total = ext[HALO:] * taps[0:1]
        for offset in range(1, TAPS):
            total = total + pltpu.roll(ext, offset, 0)[HALO:] * taps[offset : offset + 1]
        return total

    for place in range(seq_count):
        begin = place * piece
        queries_ref[:, pl.ds(begin, piece)] = branch(0, begin)
        product_ref[place] = (branch(1, begin) * branch(2, begin)).astype(jnp.bfloat16)


def short_products(projected, carried, short_filter, seq_count):
    rows, width = projected.shape[1:]
    return pl.pallas_call(
        functools.partial(short_kernel, seq_count),
        out_shape=(
            jax.ShapeDtypeStruct((rows, width), jnp.float32),
            jax.ShapeDtypeStruct((seq_count, rows, width // seq_count), jnp.bfloat16),
        ),
        in_specs=[pl.BlockSpec(memory_space=pltpu.VMEM)] * 3,
        out_specs=[pl.BlockSpec(memory_space=pltpu.VMEM)] * 2,
        compiler_params=pltpu.CompilerParams(vmem_limit_bytes=VMEM_LIMIT),
        cost_estimate=pl.CostEstimate(
            flops=20 * rows * width, bytes_accessed=12 * rows * width, transcendentals=0
        ),
        name="short_products",
    )(projected, carried, short_filter)


def mixed(terms):
    total = None
    for weight, value in terms:
        if abs(weight) < 1e-12:
            continue
        if abs(abs(weight) - 1.0) < 1e-12:
            term = value if weight > 0 else -value
        else:
            term = value * np.float32(weight)
        total = term if total is None else total + term
    return total


def conv_kernel(
    x_ref, g_ref, cos_ref, sin_ref, turn_cos_ref, turn_sin_ref, out_ref, xt, y_real, y_imag, z_real, z_imag
):
    count, rows, piece = x_ref.shape
    classes = count + 1
    freq_count = 2 * count
    total_length = freq_count * rows
    for s in range(count):
        xt[s] = x_ref[s].astype(jnp.float32).T
    for tile in range(rows // COLUMNS):
        columns = pl.ds(tile * COLUMNS, COLUMNS)
        blocks = [xt[s, :, columns] for s in range(count)]
        for r in range(classes):
            cos_r, sin_r = turn(r, freq_count, np.arange(count))
            real = mixed([(cos_r[s], blocks[s]) for s in range(count)])
            imag = mixed([(-sin_r[s], blocks[s]) for s in range(count)])
            turn_cos = turn_cos_ref[r : r + 1, columns]
            turn_sin = turn_sin_ref[r : r + 1, columns]
            if imag is None:
                turned_real, turned_imag = real * turn_cos, -(real * turn_sin)
            else:
                turned_real = real * turn_cos + imag * turn_sin
                turned_imag = imag * turn_cos - real * turn_sin
            y_real[pl.ds(r * piece, piece), columns] = turned_real.astype(jnp.bfloat16)
            y_imag[pl.ds(r * piece, piece), columns] = turned_imag.astype(jnp.bfloat16)

    def dot(a, b):
        return jnp.dot(a, b, preferred_element_type=jnp.float32)

    @pl.loop(0, rows // COLUMNS)
    def _(tile):
        columns = pl.ds(pl.multiple_of(tile * COLUMNS, COLUMNS), COLUMNS)
        table_cos, table_sin = cos_ref[:, columns], sin_ref[:, columns]
        for r in range(classes):
            place = pl.ds(r * piece, piece)
            real_in, imag_in = y_real[place], y_imag[place]
            if r == 0:
                real = dot(real_in, table_cos)
                imag = -dot(real_in, table_sin)
            else:
                real = dot(real_in, table_cos) + dot(imag_in, table_sin)
                imag = dot(imag_in, table_cos) - dot(real_in, table_sin)
            g_real = g_ref[0, r, :, columns].astype(jnp.float32)
            g_imag = g_ref[1, r, :, columns].astype(jnp.float32)
            z_real[place, columns] = (real * g_real - imag * g_imag).astype(jnp.bfloat16)
            z_imag[place, columns] = (real * g_imag + imag * g_real).astype(jnp.bfloat16)

    @pl.loop(0, rows // COLUMNS)
    def _(tile):
        columns = pl.ds(pl.multiple_of(tile * COLUMNS, COLUMNS), COLUMNS)
        table_cos, table_sin = cos_ref[:, columns], sin_ref[:, columns]
        sums = [None] * count
        for r in range(classes):
            place = pl.ds(r * piece, piece)
            real_in, imag_in = z_real[place], z_imag[place]
            real = dot(real_in, table_cos) - dot(imag_in, table_sin)
            if r == 0:
                turned_real, turned_imag = real, None
            else:
                imag = dot(imag_in, table_cos) + dot(real_in, table_sin)
                turn_cos = turn_cos_ref[r : r + 1, columns]
                turn_sin = turn_sin_ref[r : r + 1, columns]
                turned_real = real * turn_cos - imag * turn_sin
                turned_imag = imag * turn_cos + real * turn_sin
            cos_r, sin_r = turn(r, freq_count, np.arange(count))
            for s in range(count):
                terms = [(1.0, sums[s])] if sums[s] is not None else []
                terms += [(cos_r[s], turned_real), (-sin_r[s], turned_imag)]
                sums[s] = mixed(terms)
        for s in range(count):
            out_ref[s, columns, :] = (sums[s] * np.float32(1.0 / total_length)).T.astype(jnp.bfloat16)


def long_convolution(blocks, response, tables):
    count, rows, piece = blocks.shape
    classes = count + 1
    flops = (16 * classes) * piece * rows * rows
    return pl.pallas_call(
        conv_kernel,
        out_shape=jax.ShapeDtypeStruct((count, rows, piece), jnp.bfloat16),
        in_specs=[pl.BlockSpec(memory_space=pltpu.VMEM)] * 6,
        out_specs=pl.BlockSpec(memory_space=pltpu.VMEM),
        scratch_shapes=[
            pltpu.VMEM((count, piece, rows), jnp.float32),
            pltpu.VMEM((classes * piece, rows), jnp.bfloat16),
            pltpu.VMEM((classes * piece, rows), jnp.bfloat16),
            pltpu.VMEM((classes * piece, rows), jnp.bfloat16),
            pltpu.VMEM((classes * piece, rows), jnp.bfloat16),
        ],
        compiler_params=pltpu.CompilerParams(vmem_limit_bytes=VMEM_LIMIT),
        cost_estimate=pl.CostEstimate(
            flops=flops, bytes_accessed=4 * rows * rows + 4 * classes * piece * rows, transcendentals=0
        ),
        name="long_convolution",
    )(blocks, response, *tables)


def folded_response(spectrum):
    freq_count, rows = spectrum.shape[1], spectrum.shape[3]
    half = freq_count // 2
    mirror = np.eye(rows, dtype=np.float32)[::-1]
    upper = jnp.einsum(
        "ckej,jm->ckem",
        spectrum[:, half + 1 :][:, ::-1],
        jnp.asarray(mirror, jnp.bfloat16),
        preferred_element_type=jnp.float32,
    )
    upper = upper * jnp.array([1.0, -1.0], jnp.float32)[:, None, None, None]
    middle = (spectrum[:, 1:half].astype(jnp.float32) + upper).astype(jnp.bfloat16)
    return jnp.concatenate([spectrum[:, :1], middle, spectrum[:, half : half + 1]], axis=1)


def dft_tables(rows, count):
    index = np.arange(rows)
    table_cos, table_sin = turn(index[:, None], rows, index[None, :])
    classes = np.arange(count + 1)
    turn_cos, turn_sin = turn(classes[:, None], 2 * count * rows, index[None, :])
    return (
        jnp.asarray(table_cos, jnp.bfloat16),
        jnp.asarray(table_sin, jnp.bfloat16),
        jnp.asarray(turn_cos, jnp.float32),
        jnp.asarray(turn_sin, jnp.float32),
    )


def per_device(tokens, norm_gain, in_weight, short_filter, filter_spectrum, out_weight):
    seq_count = lax.axis_size("seq")
    tensor_count = lax.axis_size("tensor")
    swap = [(i, i + 1 - 2 * (i % 2)) for i in range(tensor_count)]
    other_weight = lax.ppermute(out_weight, "tensor", swap)
    inputs = tokens.astype(jnp.float32)
    square_mean = jnp.mean(inputs * inputs, axis=-1, keepdims=True)
    normed = (inputs / jnp.sqrt(square_mean + EPS) * norm_gain).astype(jnp.bfloat16)
    width = in_weight.shape[2]
    projected, spectrum = gathered_projection(
        normed,
        in_weight.transpose(1, 0, 2),
        filter_spectrum.astype(jnp.bfloat16),
        seq_count,
        tensor_count,
    )
    rows = projected.shape[1]
    tables = dft_tables(rows, seq_count)
    route = [(i, i + 1) for i in range(seq_count - 1)]
    carried = lax.ppermute(projected[:, rows - HALO :], "seq", route)
    response = folded_response(spectrum)
    queries, product = short_products(projected, carried, short_filter, seq_count)
    blocks = lax.all_to_all(product, "seq", split_axis=0, concat_axis=0, tiled=True)
    values = long_convolution(blocks, response, tables)
    returned = lax.all_to_all(values, "seq", split_axis=0, concat_axis=0, tiled=True)
    return scattered_output(tokens, queries, returned, out_weight, other_weight, tensor_count)


def solution(mesh):
    in_specs = (
        P(("seq", "tensor"), None),
        P(),
        P(None, None, "tensor"),
        P(None, None, "tensor"),
        P(None, "seq", "tensor", None),
        P("tensor", None),
    )
    out_specs = P(("seq", "tensor"), None)
    return jax.shard_map(
        per_device, mesh=mesh, in_specs=in_specs, out_specs=out_specs, check_vma=False
    )
```
